32 devices in a mesh: cast: 8 (over z, x), width: 2 (over y), thick: 2 (over core).
Axes of the slice: x: 2, y: 2, z: 4, core: 2. Of those that a mesh axis runs over, the one named last changes fastest.
Arguments:
- velocity: float32 [3, 64, 32, 256], P(None, 'cast', 'width', 'thick'), may hold values from -2 to 3.5
- magnetic: float32 [3, 64, 32, 256], P(None, 'cast', 'width', 'thick'), may hold values from -1.2 to 2.25
Outputs:
- updated_velocity: float32 [3, 64, 32, 256], P(None, 'cast', 'width', 'thick')
- potential: float32 [64, 32, 256], P('cast', 'width', 'thick')
The draws below stay inside these ranges and needn't reach their ends.
All inputs are finite; a program needn't handle non-finite values.
Results may differ from the reference program's by a relative error of at most 0.0003.
Values sent between devices are 32-bit elements; how exact they have to be, the bound alone decides.
A program may use at most 64 MiB of HBM per device.

```python
import jax
import jax.numpy as jnp

CYCLES = 2
SWEEPS = 3
LEVELS = 3
NX = 64
NY = 32
NZ = 256


def draw_velocity(key, part):
    key = jax.random.fold_in(key, 11)
    noise = 0.5 * jnp.clip(jax.random.normal(key, (3, NX, NY, NZ), jnp.float32), -4.0, 4.0)
    lowest = 0.5
    placed = (jnp.arange(NX, dtype=jnp.float32) + 0.5) / NX
    ramped = lowest + placed
    return jnp.concatenate([noise[:1] + ramped[None, :, None, None], noise[1:]], axis=0)


def draw_magnetic(key, part):
    key = jax.random.fold_in(key, 23)
    key_side, key_main = jax.random.split(key)
    sideways = 0.3 * jnp.clip(jax.random.normal(key_side, (2, NX, NY, NZ), jnp.float32), -4.0, 4.0)
    spread = jax.random.uniform(key_main, (NX, NY, NZ), jnp.float32, jnp.log(0.6), jnp.log(1.5))
    placed = (jnp.arange(NX, dtype=jnp.float32) + 0.5) / NX
    banded = 0.3 + 1.2 * jnp.exp(-((placed - 0.35) / 0.12) ** 2)
    normal_part = banded[:, None, None] * jnp.exp(spread)
    return jnp.concatenate([sideways, normal_part[None]], axis=0)


def setup_inputs(seed: int = 0) -> dict:
    keys = jax.random.split(jax.random.key(seed), 3)
    velocity = draw_velocity(jax.random.fold_in(keys[2], 71), 0)
    magnetic = draw_magnetic(jax.random.fold_in(keys[2], 71), 0)
    return dict(velocity=velocity, magnetic=magnetic)


relax_weight = 0.8
section_weight = 0.5
cast_speed = 1.0


def shifted_sum(padded):
    total = padded[2:, 1:-1, 1:-1] + padded[:-2, 1:-1, 1:-1]
    total = total + padded[1:-1, 2:, 1:-1] + padded[1:-1, :-2, 1:-1]
    return total + padded[1:-1, 1:-1, 2:] + padded[1:-1, 1:-1, :-2]


def operate(field):
    return 6.0 * field - shifted_sum(jnp.pad(field, 1))


def smooth_once(field, source):
    return field + (relax_weight / 6.0) * (source - operate(field))


def restrict(residue):
    count_x, count_y, count_z = residue.shape
    blocks = residue.reshape(count_x // 2, 2, count_y // 2, 2, count_z // 2, 2)
    return 4.0 * jnp.mean(blocks, axis=(1, 3, 5))


def prolong(coarse):
    return jnp.repeat(jnp.repeat(jnp.repeat(coarse, 2, axis=0), 2, axis=1), 2, axis=2)


def vcycle(field, source, level):
    if level == LEVELS - 1:
        for sweep_index in range(SWEEPS):
            field = smooth_once(field, source)
        return field
    for sweep_index in range(SWEEPS):
        field = smooth_once(field, source)
    residue = source - operate(field)
    reduced = restrict(residue)
    coarse = vcycle(jnp.zeros(reduced.shape, jnp.float32), reduced, level + 1)
    field = field + prolong(coarse)
    for sweep_index in range(SWEEPS):
        field = smooth_once(field, source)
    return field


def cross(left, right):
    return jnp.stack([left[1] * right[2] - left[2] * right[1],
                      left[2] * right[0] - left[0] * right[2],
                      left[0] * right[1] - left[1] * right[0]], axis=0)


def divergence(padded):
    total = padded[0, 2:, 1:-1, 1:-1] - padded[0, :-2, 1:-1, 1:-1]
    total = total + (padded[1, 1:-1, 2:, 1:-1] - padded[1, 1:-1, :-2, 1:-1])
    total = total + (padded[2, 1:-1, 1:-1, 2:] - padded[2, 1:-1, 1:-1, :-2])
    return 0.5 * total


def gradient(padded):
    return jnp.stack([0.5 * (padded[2:, 1:-1, 1:-1] - padded[:-2, 1:-1, 1:-1]),
                      0.5 * (padded[1:-1, 2:, 1:-1] - padded[1:-1, :-2, 1:-1]),
                      0.5 * (padded[1:-1, 1:-1, 2:] - padded[1:-1, 1:-1, :-2])], axis=0)


def reference(velocity, magnetic):
    electric = cross(velocity, magnetic)
    source = -divergence(jnp.pad(electric, ((0, 0), (1, 1), (1, 1), (1, 1))))
    potential = jnp.zeros(source.shape, jnp.float32)
    for cycle_index in range(CYCLES):
        potential = vcycle(potential, source, 0)
    current = electric - gradient(jnp.pad(potential, 1))
    force = cross(current, magnetic)
    moved = velocity + section_weight * force
    bulk = jnp.sum(moved[0]) / float(NX * NY * NZ)
    updated = jnp.concatenate([moved[:1] - bulk + cast_speed, moved[1:]], axis=0)
    return updated, potential
```

```python
import functools

import jax
import jax.numpy as jnp
from jax import lax
from jax.experimental import pallas as pl
from jax.experimental.pallas import tpu as pltpu
from jax.sharding import PartitionSpec as P

CYCLES = 2
weight = 0.8 / 6.0
keep = 0.2
section_weight = 0.5
cast_speed = 1.0
HIGH = lax.Precision.HIGHEST
MESH = pl.DeviceIdType.MESH

HALO0 = 12
NEAR = 4


def dot(a, b):
    return jnp.dot(a, b, precision=HIGH, preferred_element_type=jnp.float32)


def iotas(shape):
    return lax.broadcasted_iota(jnp.int32, shape, 0), lax.broadcasted_iota(jnp.int32, shape, 1)


def pair_matrix(rows, cols, fine_axis, offset=0):
    i, j = iotas((rows, cols))
    if fine_axis == 0:
        hit = lax.shift_right_logical(i, 1) + offset == j
    else:
        hit = lax.shift_right_logical(j, 1) == i
    return jnp.where(hit, 1.0, 0.0).astype(jnp.float32)


def kernel(
    counts, v_ref, b_ref, out_ref, pot_ref,
    e_ref, sblk, exl, exr, eys, eyn, ezp,
    gk, fa, fb, g1blk, g1w, f1a, f1b, r1, g2, f2a, f2b,
    s1, s2, part1, part2,
    sem_as, sem_ar, sem_bs, sem_br, sem_cs, sem_cr, sem_ps, sem_pr, sem_loc,
):
    CX, CW = counts
    X, Y, Z = sblk.shape
    Y0, Z0 = gk.shape[1], gk.shape[2]
    Y1, Y2 = g1w.shape[2], g2.shape[1]
    two = CW == 2
    c, w, t = lax.axis_index("cast"), lax.axis_index("width"), lax.axis_index("thick")
    nx0 = CX * X

    def has_x(d):
        return jnp.logical_and(c + d >= 0, c + d < CX)

    def has_w(d):
        return jnp.logical_and(w + d >= 0, w + d < CW)

    def dys(reach):
        return (0, 1) if two else tuple(range(-reach, reach + 1))

    def wid(dy):
        return lax.rem(w + dy, 2) if two else w + dy

    def when_x(dx, fn):
        if dx == 0:
            fn()
        else:
            pl.when(has_x(dx))(fn)

    def when_w(dy, fn):
        if dy == 0 or two:
            fn()
        else:
            pl.when(has_w(dy))(fn)

    for ref in (exl, exr, eyn):
        ref[...] = jnp.zeros_like(ref)

    def clear(ref, first, count, per):
        def body(i, carry):
            for j in range(per):
                ref[first + i * per + j] = jnp.zeros(ref.shape[1:], jnp.float32)
            return carry

        lax.fori_loop(0, count // per, body, 0)

    if two:
        @pl.when(jnp.logical_not(has_x(-2)))
        def _():
            clear(gk, 0, 4, 4)

        @pl.when(jnp.logical_not(has_x(-1)))
        def _():
            clear(gk, 4, 8, 4)

        @pl.when(jnp.logical_not(has_x(1)))
        def _():
            clear(gk, 20, 8, 4)

        @pl.when(jnp.logical_not(has_x(2)))
        def _():
            clear(gk, 28, 4, 4)

        for n in range(CYCLES):
            for dx in range(-NEAR, NEAR + 1):
                if dx:
                    @pl.when(jnp.logical_not(has_x(dx)))
                    def _(n=n, dx=dx):
                        clear(g1w.at[n], 4 * (NEAR + dx), 4, 4)
    else:
        clear(gk, 0, gk.shape[0], 4)
        for n in range(CYCLES):
            clear(g1w.at[n], 0, g1w.shape[1], 4)

    barrier = pltpu.get_barrier_semaphore()
    need = jnp.int32(CX - 1)
    for d in range(1, CX):
        pl.semaphore_signal(barrier, 1, device_id=(lax.rem(c + d, CX), w, t), device_id_type=MESH)
    all_w = (0, 1) if two else tuple(range(-(CW - 1), CW))
    far = NEAR
    for dx in range(-far, far + 1):
        for dy in all_w:
            for dt in (0, 1):
                if dy == 0 and dt == 0:
                    continue
                wide = abs(dx) <= 2 and (two or abs(dy) <= 1)
                coarse = dt == 0 and (two or abs(dy) <= 2)
                if not (wide or coarse or dx == 0):
                    continue
                ok = jnp.bool_(True)
                if dx:
                    ok = jnp.logical_and(ok, has_x(dx))
                if dy and not two:
                    ok = jnp.logical_and(ok, has_w(dy))

                def greet(dx=dx, dy=dy, dt=dt):
                    pl.semaphore_signal(
                        barrier, 1, device_id=(c + dx, wid(dy), lax.rem(t + dt, 2)), device_id_type=MESH
                    )

                if dx == 0 and (dy == 0 or two):
                    greet()
                    need = need + 1
                else:
                    pl.when(ok)(greet)
                    need = need + jnp.where(ok, 1, 0).astype(jnp.int32)

    for i in range(X):
        v0, v1, v2 = v_ref[0, i], v_ref[1, i], v_ref[2, i]
        b0, b1, b2 = b_ref[0, i], b_ref[1, i], b_ref[2, i]
        e_ref[0, i] = v1 * b2 - v2 * b1
        ey = v2 * b0 - v0 * b2
        e_ref[1, i] = ey
        eys[0, i : i + 1, :] = ey[0:1, :]
        eys[1, i : i + 1, :] = ey[Y - 1 : Y, :]
        e_ref[2, i] = v0 * b1 - v1 * b0

    pl.semaphore_wait(barrier, need)

    def copy_a(k):
        if k == 0:
            args = (e_ref.at[0, X - 1], exl, (c + 1, w, t))
        elif k == 1:
            args = (e_ref.at[0, 0], exr, (c - 1, w, t))
        elif k == 2:
            args = (eys.at[1], eyn.at[0], (c, w + 1, t))
        elif k == 3:
            args = (eys.at[0], eyn.at[1], (c, w - 1, t))
        else:
            args = (e_ref.at[2], ezp, (c, w, 1 - t))
        return pltpu.make_async_remote_copy(
            args[0], args[1], sem_as.at[k], sem_ar.at[k], device_id=args[2], device_id_type=MESH
        )

    send_ok = (has_x(1), has_x(-1), has_w(1), has_w(-1))
    recv_ok = (has_x(-1), has_x(1), has_w(-1), has_w(1))
    for k in range(4):
        pl.when(send_ok[k])(lambda k=k: copy_a(k).start())
    copy_a(4).start()
    for k in range(4):
        pl.when(recv_ok[k])(lambda k=k: copy_a(k).wait_recv())
    copy_a(4).wait_recv()

    row, lane = iotas((Y, Z))
    for i in range(X):
        ex0 = e_ref[0, i - 1] if i else exl[...]
        ex1 = e_ref[0, i + 1] if i < X - 1 else exr[...]
        ey, ez, pz = e_ref[1, i], e_ref[2, i], ezp[i]
        ey1 = jnp.where(row == Y - 1, eyn[1, i : i + 1, :], pltpu.roll(ey, Y - 1, 0))
        ey0 = jnp.where(row == 0, eyn[0, i : i + 1, :], pltpu.roll(ey, 1, 0))
        edge1 = jnp.where(t == 0, pltpu.roll(pz, Z - 1, 1), 0.0)
        edge0 = jnp.where(t == 0, 0.0, pltpu.roll(pz, 1, 1))
        ez1 = jnp.where(lane == Z - 1, edge1, pltpu.roll(ez, Z - 1, 1))
        ez0 = jnp.where(lane == 0, edge0, pltpu.roll(ez, 1, 1))
        sblk[i] = (-0.5 * weight) * ((ex1 - ex0) + (ey1 - ey0) + (ez1 - ez0))

    def rows_b(dy):
        return pl.ds(pl.multiple_of(w * Y, Y), Y) if two else pl.ds((1 - dy) * Y, Y)

    my_lanes = pl.ds(pl.multiple_of(t * Z, Z), Z)
    ydys = dys(1)

    def copy_b(dx, dy, dt):
        if dx == 2:
            src, dst = (4, 4), 0
        elif dx == -2:
            src, dst = (0, 4), HALO0 + X + X
        else:
            src, dst = (0, X), HALO0 - dx * X
        k = ((dx + 2) * len(ydys) + ydys.index(dy)) * 2 + dt
        return pltpu.make_async_remote_copy(
            sblk.at[pl.ds(src[0], src[1])],
            gk.at[pl.ds(dst, src[1]), rows_b(dy), my_lanes],
            sem_bs.at[k], sem_br.at[k],
            device_id=(c + dx, wid(dy), lax.rem(t + dt, 2)), device_id_type=MESH,
        )

    def each_b(fn, sign):
        for dx in (1, -1, 2, -2, 0):
            def run(dx=dx):
                for dy in ydys:
                    def run_w(dy=dy):
                        for dt in (0, 1):
                            if dx or dy or dt:
                                fn(copy_b(dx, dy, dt))

                    if two:
                        run_w()
                    else:
                        when_w(sign * dy, run_w)

            when_x(sign * dx, run)

    each_b(lambda d: d.start(), 1)
    own = pltpu.make_async_copy(
        sblk, gk.at[pl.ds(HALO0, X), pl.ds(pl.multiple_of(w * Y, Y), Y) if two else pl.ds(Y, Y), my_lanes],
        sem_loc.at[0],
    )
    own.start()
    own.wait()
    each_b(lambda d: d.wait_recv(), -1)

    def neighbours(v):
        ny, nz = v.shape
        r, l = iotas(v.shape)
        total = jnp.where(r == 0, 0.0, pltpu.roll(v, 1, 0)) + jnp.where(r == ny - 1, 0.0, pltpu.roll(v, ny - 1, 0))
        total = total + jnp.where(l == 0, 0.0, pltpu.roll(v, 1, 1))
        return total + jnp.where(l == nz - 1, 0.0, pltpu.roll(v, nz - 1, 1))

    def factor(plane, first, count, shape, lev):
        g = first + plane
        k = jnp.where(jnp.logical_and(g >= 0, g < count), weight, 0.0).astype(jnp.float32)
        if not two:
            base = (w * Y - Y, w * (Y // 2) - Y, w * (Y // 4) - Y // 2)[lev]
            size = (CW * Y, CW * (Y // 2), CW * (Y // 4))[lev]
            r, _ = iotas(shape)
            k = jnp.where(jnp.logical_and(r + base >= 0, r + base < size), k, 0.0)
        if lev == 2:
            _, l = iotas(shape)
            k = jnp.where(l < Z0 // 4, k, 0.0)
        return k

    def apply(lev, src, g, dst, lo, hi, residual=False, last=None):
        first = (c * X - HALO0, c * (X // 2) - NEAR * (X // 2), c * (X // 4) - NEAR * (X // 4))[lev]
        count = nx0 >> lev
        n = hi - lo
        step = max(d for d in ((1, 2) if lev == 0 else (1, 2, 3, 4, 5)) if n % d == 0)

        def body(i, carry):
            p = lo + i * step
            v = [src[p - 1 + j] for j in range(step + 2)]
            for j in range(step):
                mid = v[j + 1]
                nb = v[j] + v[j + 2] + neighbours(mid)
                k = factor(p + j, first, count, mid.shape, lev)
                if residual:
                    dst[p + j] = g[p + j] + k * nb - 0.8 * mid
                else:
                    dst[p + j] = keep * mid + k * nb + g[p + j]
            return carry

        lax.fori_loop(0, n // step, body, 0)

    def own_rows(v):
        return jnp.where(w == 0, v[:Y], v[Y:]) if two else v[Y : 2 * Y]

    def own_lanes(v):
        return jnp.where(t == 0, v[:, :Z], v[:, Z:])

    H1 = NEAR * (X // 2)
    H2 = NEAR * (X // 4)
    pz0 = pair_matrix(Z0, Z0 // 2, 0)
    pz1 = pair_matrix(Z0 // 2, Z0 // 2, 0)
    uz0 = pair_matrix(Z0 // 2, Z0, 1)
    uz1 = pair_matrix(Z0 // 2, Z0 // 2, 1)
    py0 = pair_matrix(Y // 2, Y, 1)
    py1 = pair_matrix(Y2, Y1, 1)
    uy1 = pair_matrix(Y1, Y2, 0)
    uy0 = pair_matrix(Y0, Y1, 0, 0 if two else Y // 2)

    cdys = dys(2)

    def rows_c(dy):
        half = Y // 2
        return pl.ds(pl.multiple_of(w * half, half), half) if two else pl.ds((2 - dy) * half, half)

    def copy_c(n, dx, dy):
        k = (dx + NEAR) * len(cdys) + cdys.index(dy)
        return pltpu.make_async_remote_copy(
            g1blk.at[n], g1w.at[n, pl.ds((NEAR - dx) * (X // 2), X // 2), rows_c(dy)],
            sem_cs.at[n, k], sem_cr.at[n, k],
            device_id=(c + dx, wid(dy), t), device_id_type=MESH,
        )

    def each_c(n, fn, sign):
        for dx in (4, -4, 3, -3, 2, -2, 1, -1, 0):
            def run(dx=dx):
                for dy in cdys:
                    if dx or dy:
                        when_w(sign * dy, lambda dy=dy: fn(copy_c(n, dx, dy)))

            when_x(sign * dx, run)

    def coarse(n, src, out0):
        apply(0, src, gk, fb, HALO0, HALO0 + X, residual=True)
        sums = [own_rows(fb[HALO0 + 2 * i] + fb[HALO0 + 2 * i + 1]) for i in range(X // 2)]
        flat = 0.5 * dot(jnp.concatenate(sums, axis=0), pz0)
        for i in range(X // 2):
            g1blk[n, i] = dot(py0, flat[i * Y : (i + 1) * Y])
        each_c(n, lambda d: d.start(), 1)
        mine = pltpu.make_async_copy(
            g1blk.at[n], g1w.at[n, pl.ds(H1, X // 2), rows_c(0)], sem_loc.at[1 + n]
        )
        mine.start()
        mine.wait()
        each_c(n, lambda d: d.wait_recv(), -1)

        g1 = g1w.at[n]
        B1, B2 = X // 2, X // 4
        h8 = out0 + 3
        h4 = (h8 + 1) // 2
        h6 = h4 + 2
        h12 = 2 * h6
        apply(1, g1, g1, f1b, H1 - h12 - 2, H1 + B1 + h12 + 2)
        apply(1, f1b, g1, f1a, H1 - h12 - 1, H1 + B1 + h12 + 1)
        apply(1, f1a, g1, r1, H1 - h12, H1 + B1 + h12, residual=True)
        m = B2 + 2 * h6
        lo = H1 - h12
        half = [r1[lo + 2 * i] + r1[lo + 2 * i + 1] for i in range(m)]
        flat = 0.5 * dot(jnp.concatenate(half, axis=0), pz1)
        for i in range(m):
            g2[H2 - h6 + i] = dot(py1, flat[i * Y1 : (i + 1) * Y1])
        apply(2, g2, g2, f2b, H2 - h6 + 1, H2 + B2 + h6 - 1)
        apply(2, f2b, g2, f2a, H2 - h4, H2 + B2 + h4)
        m = B2 + 2 * h4
        flat = dot(jnp.concatenate([f2a[H2 - h4 + i] for i in range(m)], axis=0), uz1)
        for i in range(m):
            up = dot(uy1, flat[i * Y2 : (i + 1) * Y2])
            p = H1 - 2 * h4 + 2 * i
            f1a[p] = f1a[p] + up
            f1a[p + 1] = f1a[p + 1] + up
        apply(1, f1a, g1, f1b, H1 - out0 - 2, H1 + B1 + out0 + 2)
        apply(1, f1b, g1, f1a, H1 - out0 - 1, H1 + B1 + out0 + 1)
        apply(1, f1a, g1, f1b, H1 - out0, H1 + B1 + out0)
        m = B1 + 2 * out0
        flat = dot(jnp.concatenate([f1b[H1 - out0 + i] for i in range(m)], axis=0), uz0)
        for i in range(m):
            up = dot(uy0, flat[i * Y1 : (i + 1) * Y1])
            p = HALO0 - 2 * out0 + 2 * i
            src[p] = src[p] + up
            src[p + 1] = src[p + 1] + up

    def at(h):
        return HALO0 - h, HALO0 + X + h

    apply(0, gk, gk, fb, *at(11))
    apply(0, fb, gk, fa, *at(10))
    coarse(0, fa, 5)
    apply(0, fa, gk, fb, *at(9))
    apply(0, fb, gk, fa, *at(8))
    apply(0, fa, gk, fb, *at(7))
    apply(0, fb, gk, fa, *at(6))
    apply(0, fa, gk, fb, *at(5))
    apply(0, fb, gk, fa, *at(4))
    coarse(1, fa, 2)
    apply(0, fa, gk, fb, *at(3))
    apply(0, fb, gk, fa, *at(2))
    apply(0, fa, gk, fb, *at(1))

    acc = jnp.zeros((Y, Z), jnp.float32)
    r0, l0 = iotas((Y0, Z0))
    for i in range(X):
        p = HALO0 + i
        mid = fb[p]
        pot_ref[i] = own_lanes(own_rows(mid))
        j0 = 0.5 * own_lanes(own_rows(fb[p + 1] - fb[p - 1]))
        dy = jnp.where(r0 == Y0 - 1, 0.0, pltpu.roll(mid, Y0 - 1, 0)) - jnp.where(r0 == 0, 0.0, pltpu.roll(mid, 1, 0))
        dz = jnp.where(l0 == Z0 - 1, 0.0, pltpu.roll(mid, Z0 - 1, 1)) - jnp.where(l0 == 0, 0.0, pltpu.roll(mid, 1, 1))
        c0 = e_ref[0, i] - j0
        c1 = e_ref[1, i] - 0.5 * own_lanes(own_rows(dy))
        c2 = e_ref[2, i] - 0.5 * own_lanes(own_rows(dz))
        b0, b1, b2 = b_ref[0, i], b_ref[1, i], b_ref[2, i]
        m0 = v_ref[0, i] + section_weight * (c1 * b2 - c2 * b1)
        out_ref[0, i] = m0
        acc = acc + m0
        out_ref[1, i] = v_ref[1, i] + section_weight * (c2 * b0 - c0 * b2)
        out_ref[2, i] = v_ref[2, i] + section_weight * (c0 * b1 - c1 * b0)

    s1[...] = acc[:8] + acc[8:]
    pairs = [(dw, dt) for dw in range(CW) for dt in (0, 1)]

    def copy_p(k):
        dw, dt = pairs[k]
        return pltpu.make_async_remote_copy(
            s1, part1.at[k], sem_ps.at[k], sem_pr.at[k],
            device_id=(c, lax.rem(w + dw, CW), lax.rem(t + dt, 2)), device_id_type=MESH,
        )

    def copy_q(d):
        k = len(pairs) + d
        return pltpu.make_async_remote_copy(
            s2, part2.at[d], sem_ps.at[k], sem_pr.at[k],
            device_id=(lax.rem(c + d, CX), w, t), device_id_type=MESH,
        )

    for k in range(1, len(pairs)):
        copy_p(k).start()
    total = s1[...]
    for k in range(1, len(pairs)):
        copy_p(k).wait_recv()
        total = total + part1[k]
    s2[...] = total
    for d in range(1, CX):
        copy_q(d).start()
    for d in range(1, CX):
        copy_q(d).wait_recv()
        total = total + part2[d]
    bulk = jnp.sum(total) * (1.0 / float(nx0 * CW * Y * Z0))
    for i in range(X):
        out_ref[0, i] = out_ref[0, i] - bulk + cast_speed

    for k in range(4):
        pl.when(send_ok[k])(lambda k=k: copy_a(k).wait_send())
    copy_a(4).wait_send()
    each_b(lambda d: d.wait_send(), 1)
    for n in range(CYCLES):
        each_c(n, lambda d: d.wait_send(), 1)
    for k in range(1, len(pairs)):
        copy_p(k).wait_send()
    for d in range(1, CX):
        copy_q(d).wait_send()


def solution(mesh):
    CX, CW = mesh.shape["cast"], mesh.shape["width"]

    def per_device(velocity, magnetic):
        _, X, Y, Z = velocity.shape
        two = CW == 2
        Y0 = 2 * Y if two else 3 * Y
        Y1 = Y if two else 5 * (Y // 2)
        Y2 = -(-(Y1 // 2) // 8) * 8
        Z0 = 2 * Z
        N0, N1, N2 = X + 2 * HALO0, (X // 2) * (2 * NEAR + 1), (X // 4) * (2 * NEAR + 1)
        nb, nc = 5 * (2 if two else 3) * 2, (2 * NEAR + 1) * (2 if two else 5)
        np_ = 2 * CW + CX
        f32 = jnp.float32
        V = pltpu.VMEM
        D = pltpu.SemaphoreType.DMA
        return pl.pallas_call(
            functools.partial(kernel, (CX, CW)),
            out_shape=(
                jax.ShapeDtypeStruct((3, X, Y, Z), f32),
                jax.ShapeDtypeStruct((X, Y, Z), f32),
            ),
            in_specs=[pl.BlockSpec(memory_space=V)] * 2,
            out_specs=(pl.BlockSpec(memory_space=V),) * 2,
            scratch_shapes=[
                V((3, X, Y, Z), f32), V((X, Y, Z), f32), V((Y, Z), f32), V((Y, Z), f32),
                V((2, X, Z), f32), V((2, X, Z), f32), V((X, Y, Z), f32),
                V((N0, Y0, Z0), f32), V((N0, Y0, Z0), f32), V((N0, Y0, Z0), f32),
                V((CYCLES, X // 2, Y // 2, Z), f32), V((CYCLES, N1, Y1, Z), f32),
                V((N1, Y1, Z), f32), V((N1, Y1, Z), f32), V((N1, Y1, Z), f32),
                V((N2, Y2, Z), f32), V((N2, Y2, Z), f32), V((N2, Y2, Z), f32),
                V((8, Z), f32), V((8, Z), f32), V((2 * CW, 8, Z), f32), V((CX, 8, Z), f32),
                D((5,)), D((5,)), D((nb,)), D((nb,)), D((CYCLES, nc)), D((CYCLES, nc)),
                D((np_,)), D((np_,)), D((1 + CYCLES,)),
            ],
            compiler_params=pltpu.CompilerParams(
                collective_id=0, has_side_effects=True, vmem_limit_bytes=40 * 1024 * 1024
            ),
        )(velocity, magnetic)

    placed = (P(None, "cast", "width", "thick"), P(None, "cast", "width", "thick"))
    return jax.shard_map(
        per_device,
        mesh=mesh,
        in_specs=placed,
        out_specs=(P(None, "cast", "width", "thick"), P("cast", "width", "thick")),
        check_vma=False,
    )
```

```python
import functools

import jax
import jax.numpy as jnp
from jax import lax
from jax.experimental import pallas as pl
from jax.experimental.pallas import tpu as pltpu
from jax.sharding import PartitionSpec as P

CYCLES = 2
weight = 0.8 / 6.0
keep = 0.2
section_weight = 0.5
cast_speed = 1.0
MESH = pl.DeviceIdType.MESH

HALO0 = 12
NEAR = 4


def pieces(a):
    high = a.astype(jnp.bfloat16)
    rest = a - high.astype(jnp.float32)
    mid = rest.astype(jnp.bfloat16)
    low = (rest - mid.astype(jnp.float32)).astype(jnp.bfloat16)
    return high, mid, low


def dot(a, b):
    if a.dtype == jnp.bfloat16:
        parts = [jnp.dot(a, q, preferred_element_type=jnp.float32) for q in pieces(b)]
    else:
        parts = [jnp.dot(q, b, preferred_element_type=jnp.float32) for q in pieces(a)]
    return parts[0] + (parts[1] + parts[2])


def iotas(shape):
    return lax.broadcasted_iota(jnp.int32, shape, 0), lax.broadcasted_iota(jnp.int32, shape, 1)


def pair_matrix(rows, cols, fine_axis, offset=0):
    i, j = iotas((rows, cols))
    if fine_axis == 0:
        hit = lax.shift_right_logical(i, 1) + offset == j
    else:
        hit = lax.shift_right_logical(j, 1) == i
    return jnp.where(hit, 1.0, 0.0).astype(jnp.bfloat16)


def kernel(
    counts, v_ref, b_ref, out_ref, pot_ref,
    e_ref, sblk, exl, exr, eys, eyn, ezp,
    gk, fa, fb, g1blk, g1w, f1a, f1b, r1, g2, f2a, f2b,
    s1, s2, part1, part2,
    sem_as, sem_ar, sem_bs, sem_br, sem_cs, sem_cr, sem_ps, sem_pr, sem_loc,
):
    CX, CW = counts
    X, Y, Z = sblk.shape
    Y0, Z0 = gk.shape[1], gk.shape[2]
    Y1, Y2 = g1w.shape[2], g2.shape[1]
    two = CW == 2
    c, w, t = lax.axis_index("cast"), lax.axis_index("width"), lax.axis_index("thick")
    nx0 = CX * X

    def has_x(d):
        return jnp.logical_and(c + d >= 0, c + d < CX)

    def has_w(d):
        return jnp.logical_and(w + d >= 0, w + d < CW)

    def dys(reach):
        return (0, 1) if two else tuple(range(-reach, reach + 1))

    def wid(dy):
        return lax.rem(w + dy, 2) if two else w + dy

    def when_x(dx, fn):
        if dx == 0:
            fn()
        else:
            pl.when(has_x(dx))(fn)

    def when_w(dy, fn):
        if dy == 0 or two:
            fn()
        else:
            pl.when(has_w(dy))(fn)

    for ref in (exl, exr, eyn):
        ref[...] = jnp.zeros_like(ref)

    def clear(ref, first, count, per):
        def body(i, carry):
            for j in range(per):
                ref[first + i * per + j] = jnp.zeros(ref.shape[1:], jnp.float32)
            return carry

        lax.fori_loop(0, count // per, body, 0)

    if not two:
        clear(gk, 0, gk.shape[0], 4)
        for n in range(CYCLES):
            clear(g1w.at[n], 0, g1w.shape[1], 4)

    barrier = pltpu.get_barrier_semaphore()
    need = jnp.int32(CX - 1)
    for d in range(1, CX):
        pl.semaphore_signal(barrier, 1, device_id=(lax.rem(c + d, CX), w, t), device_id_type=MESH)
    all_w = (0, 1) if two else tuple(range(-(CW - 1), CW))
    far = NEAR
    for dx in range(-far, far + 1):
        for dy in all_w:
            for dt in (0, 1):
                if dy == 0 and dt == 0:
                    continue
                near = dt == 0 and (two or abs(dy) <= 2)
                if not (near or dx == 0):
                    continue
                ok = jnp.bool_(True)
                if dx:
                    ok = jnp.logical_and(ok, has_x(dx))
                if dy and not two:
                    ok = jnp.logical_and(ok, has_w(dy))

                def greet(dx=dx, dy=dy, dt=dt):
                    pl.semaphore_signal(
                        barrier, 1, device_id=(c + dx, wid(dy), lax.rem(t + dt, 2)), device_id_type=MESH
                    )

                if dx == 0 and (dy == 0 or two):
                    greet()
                    need = need + 1
                else:
                    pl.when(ok)(greet)
                    need = need + jnp.where(ok, 1, 0).astype(jnp.int32)

    if two:
        @pl.when(jnp.logical_not(has_x(-2)))
        def _():
            clear(gk, 0, 4, 4)

        @pl.when(jnp.logical_not(has_x(-1)))
        def _():
            clear(gk, 4, 8, 4)

        @pl.when(jnp.logical_not(has_x(1)))
        def _():
            clear(gk, 20, 8, 4)

        @pl.when(jnp.logical_not(has_x(2)))
        def _():
            clear(gk, 28, 4, 4)

        for n in range(CYCLES):
            for dx in range(-NEAR, NEAR + 1):
                if dx:
                    @pl.when(jnp.logical_not(has_x(dx)))
                    def _(n=n, dx=dx):
                        clear(g1w.at[n], 4 * (NEAR + dx), 4, 4)

    for i in range(X):
        v0, v1, v2 = v_ref[0, i], v_ref[1, i], v_ref[2, i]
        b0, b1, b2 = b_ref[0, i], b_ref[1, i], b_ref[2, i]
        e_ref[0, i] = v1 * b2 - v2 * b1
        ey = v2 * b0 - v0 * b2
        e_ref[1, i] = ey
        eys[0, i : i + 1, :] = ey[0:1, :]
        eys[1, i : i + 1, :] = ey[Y - 1 : Y, :]
        e_ref[2, i] = v0 * b1 - v1 * b0

    pl.semaphore_wait(barrier, need)

    def copy_a(k):
        if k == 0:
            args = (e_ref.at[0, X - 1], exl, (c + 1, w, t))
        elif k == 1:
            args = (e_ref.at[0, 0], exr, (c - 1, w, t))
        elif k == 2:
            args = (eys.at[1], eyn.at[0], (c, w + 1, t))
        elif k == 3:
            args = (eys.at[0], eyn.at[1], (c, w - 1, t))
        else:
            args = (e_ref.at[2], ezp, (c, w, 1 - t))
        return pltpu.make_async_remote_copy(
            args[0], args[1], sem_as.at[k], sem_ar.at[k], device_id=args[2], device_id_type=MESH
        )

    send_ok = (has_x(1), has_x(-1), has_w(1), has_w(-1))
    recv_ok = (has_x(-1), has_x(1), has_w(-1), has_w(1))
    for k in range(4):
        pl.when(send_ok[k])(lambda k=k: copy_a(k).start())
    copy_a(4).start()
    for k in range(4):
        pl.when(recv_ok[k])(lambda k=k: copy_a(k).wait_recv())
    copy_a(4).wait_recv()

    row, lane = iotas((Y, Z))
    for i in range(X):
        ex0 = e_ref[0, i - 1] if i else exl[...]
        ex1 = e_ref[0, i + 1] if i < X - 1 else exr[...]
        ey, ez, pz = e_ref[1, i], e_ref[2, i], ezp[i]
        ey1 = jnp.where(row == Y - 1, eyn[1, i : i + 1, :], pltpu.roll(ey, Y - 1, 0))
        ey0 = jnp.where(row == 0, eyn[0, i : i + 1, :], pltpu.roll(ey, 1, 0))
        edge1 = jnp.where(t == 0, pltpu.roll(pz, Z - 1, 1), 0.0)
        edge0 = jnp.where(t == 0, 0.0, pltpu.roll(pz, 1, 1))
        ez1 = jnp.where(lane == Z - 1, edge1, pltpu.roll(ez, Z - 1, 1))
        ez0 = jnp.where(lane == 0, edge0, pltpu.roll(ez, 1, 1))
        sblk[i] = (-0.5 * weight) * ((ex1 - ex0) + (ey1 - ey0) + (ez1 - ez0))

    def rows_b(dy):
        return pl.ds(pl.multiple_of(w * Y, Y), Y) if two else pl.ds((1 - dy) * Y, Y)

    my_lanes = pl.ds(pl.multiple_of(t * Z, Z), Z)
    ydys = dys(1)
    other = (c, w, 1 - t)
    mid = [(0, 0, X, HALO0)]
    near = mid + [(1, X - 4, 4, HALO0 - 4), (-1, 0, 4, HALO0 + X)]
    far = [
        (1, 0, 4, HALO0 - 8), (-1, X - 4, 4, HALO0 + X + 4),
        (2, X - 4, 4, HALO0 - 12), (-2, 0, 4, HALO0 + X + 8),
    ]
    steps = near + far

    def slot_b(entry, dy):
        return steps.index(entry) * len(ydys) + ydys.index(dy)

    def rows_in(dy, size, reach):
        return pl.ds(pl.multiple_of(wid(dy) * size, size), size) if two else pl.ds((reach - dy) * size, size)

    def copy_b(entry, dy):
        dx, first, count, land = entry
        k = slot_b(entry, dy)
        return pltpu.make_async_remote_copy(
            sblk.at[pl.ds(first, count)],
            gk.at[pl.ds(land, count), rows_b(dy), my_lanes],
            sem_bs.at[0, k], sem_br.at[0, k],
            device_id=(c + dx, wid(dy), t), device_id_type=MESH,
        )

    def pass_b(entry, dy):
        _, _, count, land = entry
        k = slot_b(entry, dy)
        place = gk.at[pl.ds(land, count), rows_in(dy, Y, 1), my_lanes]
        src = sblk if entry[0] == 0 and dy == 0 else place
        return pltpu.make_async_remote_copy(
            src, place, sem_bs.at[1, k], sem_br.at[1, k], device_id=other, device_id_type=MESH
        )

    def each_b(entries, fn, sign):
        for entry in entries:
            def run(entry=entry):
                for dy in ydys:
                    when_w(sign * dy, lambda dy=dy: fn(entry, dy))

            when_x(sign * entry[0], run)

    def is_own(entry, dy):
        return entry[0] == 0 and dy == 0

    def start_b(entry, dy):
        if not is_own(entry, dy):
            copy_b(entry, dy).start()

    def hand_on(entry, dy):
        if not is_own(entry, dy):
            copy_b(entry, dy).wait_recv()
            pass_b(entry, dy).start()

    def leave_b(entry, dy):
        if not is_own(entry, dy):
            copy_b(entry, dy).wait_send()

    each_b(steps, start_b, 1)
    pass_b(mid[0], 0).start()
    own = pltpu.make_async_copy(
        sblk, gk.at[pl.ds(HALO0, X), pl.ds(pl.multiple_of(w * Y, Y), Y) if two else pl.ds(Y, Y), my_lanes],
        sem_loc.at[0],
    )
    own.start()
    own.wait()
    each_b(near, hand_on, -1)
    each_b(near, lambda entry, dy: pass_b(entry, dy).wait_recv(), -1)

    def neighbours(v):
        ny, nz = v.shape
        r, l = iotas(v.shape)
        total = jnp.where(r == 0, 0.0, pltpu.roll(v, 1, 0)) + jnp.where(r == ny - 1, 0.0, pltpu.roll(v, ny - 1, 0))
        total = total + jnp.where(l == 0, 0.0, pltpu.roll(v, 1, 1))
        return total + jnp.where(l == nz - 1, 0.0, pltpu.roll(v, nz - 1, 1))

    def factor(plane, first, count, shape, lev):
        g = first + plane
        k = jnp.where(jnp.logical_and(g >= 0, g < count), weight, 0.0).astype(jnp.float32)
        if not two:
            base = (w * Y - Y, w * (Y // 2) - Y, w * (Y // 4) - Y // 2)[lev]
            size = (CW * Y, CW * (Y // 2), CW * (Y // 4))[lev]
            r, _ = iotas(shape)
            k = jnp.where(jnp.logical_and(r + base >= 0, r + base < size), k, 0.0)
        if lev == 2:
            _, l = iotas(shape)
            k = jnp.where(l < Z0 // 4, k, 0.0)
        return k

    def apply(lev, src, g, dst, lo, hi, residual=False, last=None):
        first = (c * X - HALO0, c * (X // 2) - NEAR * (X // 2), c * (X // 4) - NEAR * (X // 4))[lev]
        count = nx0 >> lev
        n = hi - lo
        step = max(d for d in ((1, 2, 3, 4, 5) if lev == 0 else (1, 2, 3, 4, 5, 6, 7, 8)) if n % d == 0)

        def body(i, carry):
            p = lo + i * step
            v = [src[p - 1 + j] for j in range(step + 2)]
            for j in range(step):
                mid = v[j + 1]
                nb = v[j] + v[j + 2] + neighbours(mid)
                k = factor(p + j, first, count, mid.shape, lev)
                if residual:
                    dst[p + j] = g[p + j] + k * nb - 0.8 * mid
                else:
                    dst[p + j] = keep * mid + k * nb + g[p + j]
            return carry

        lax.fori_loop(0, n // step, body, 0)

    def own_rows(v):
        return jnp.where(w == 0, v[:Y], v[Y:]) if two else v[Y : 2 * Y]

    def own_lanes(v):
        return jnp.where(t == 0, v[:, :Z], v[:, Z:])

    H1 = NEAR * (X // 2)
    H2 = NEAR * (X // 4)
    pz0 = pair_matrix(Z0, Z0 // 2, 0)
    pz1 = pair_matrix(Z0 // 2, Z0 // 2, 0)
    uz0 = pair_matrix(Z0 // 2, Z0, 1)
    uz1 = pair_matrix(Z0 // 2, Z0 // 2, 1)
    py0 = pair_matrix(Y // 2, Y, 1)
    py1 = pair_matrix(Y2, Y1, 1)
    uy1 = pair_matrix(Y1, Y2, 0)
    uy0 = pair_matrix(Y0, Y1, 0, 0 if two else Y // 2)

    cdys = dys(2)

    def rows_c(dy):
        half = Y // 2
        return pl.ds(pl.multiple_of(w * half, half), half) if two else pl.ds((2 - dy) * half, half)

    part = X // 4

    def copy_c(n, dx, dy):
        k = (dx + NEAR) * len(cdys) + cdys.index(dy)
        return pltpu.make_async_remote_copy(
            g1blk.at[n, pl.ds(t * part, part)],
            g1w.at[n, pl.ds((NEAR - dx) * (X // 2) + t * part, part), rows_c(dy)],
            sem_cs.at[n, 0, k], sem_cr.at[n, 0, k],
            device_id=(c + dx, wid(dy), t), device_id_type=MESH,
        )

    def pass_c(n, dx, dy):
        k = (dx + NEAR) * len(cdys) + cdys.index(dy)
        place = g1w.at[n, pl.ds((NEAR - dx) * (X // 2) + t * part, part), rows_in(dy, Y // 2, 2)]
        return pltpu.make_async_remote_copy(
            place, place, sem_cs.at[n, 1, k], sem_cr.at[n, 1, k], device_id=other, device_id_type=MESH
        )

    def each_c(n, fn, sign, order):
        for dx in order:
            def run(dx=dx):
                for dy in cdys:
                    if dx or dy:
                        when_w(sign * dy, lambda dy=dy: fn(n, dx, dy))

            when_x(sign * dx, run)

    outward = (0, 1, -1, 2, -2, 3, -3, 4, -4)

    def hand_on_c(n, dx, dy):
        copy_c(n, dx, dy).wait_recv()
        pass_c(n, dx, dy).start()

    def coarse(n, src, out0, between):
        apply(0, src, gk, fb, HALO0, HALO0 + X, residual=True)
        sums = [own_rows(fb[HALO0 + 2 * i] + fb[HALO0 + 2 * i + 1]) for i in range(X // 2)]
        flat = 0.5 * dot(jnp.concatenate(sums, axis=0), pz0)
        for i in range(X // 2):
            g1blk[n, i] = dot(py0, flat[i * Y : (i + 1) * Y])
        each_c(n, lambda *a: copy_c(*a).start(), 1, outward[::-1])
        mine = pltpu.make_async_copy(
            g1blk.at[n], g1w.at[n, pl.ds(H1, X // 2), rows_c(0)], sem_loc.at[1 + n]
        )
        mine.start()
        mine.wait()
        between()
        each_c(n, hand_on_c, -1, outward)
        each_c(n, lambda *a: pass_c(*a).wait_recv(), -1, outward)

        g1 = g1w.at[n]
        B1, B2 = X // 2, X // 4
        h8 = out0 + 3
        h4 = (h8 + 1) // 2
        h6 = h4 + 2
        h12 = 2 * h6
        apply(1, g1, g1, f1b, H1 - h12 - 2, H1 + B1 + h12 + 2)
        apply(1, f1b, g1, f1a, H1 - h12 - 1, H1 + B1 + h12 + 1)
        apply(1, f1a, g1, r1, H1 - h12, H1 + B1 + h12, residual=True)
        m = B2 + 2 * h6
        lo = H1 - h12
        half = [r1[lo + 2 * i] + r1[lo + 2 * i + 1] for i in range(m)]
        flat = 0.5 * dot(jnp.concatenate(half, axis=0), pz1)
        for i in range(m):
            g2[H2 - h6 + i] = dot(py1, flat[i * Y1 : (i + 1) * Y1])
        apply(2, g2, g2, f2b, H2 - h6 + 1, H2 + B2 + h6 - 1)
        apply(2, f2b, g2, f2a, H2 - h4, H2 + B2 + h4)
        m = B2 + 2 * h4
        flat = dot(jnp.concatenate([f2a[H2 - h4 + i] for i in range(m)], axis=0), uz1)
        for i in range(m):
            up = dot(uy1, flat[i * Y2 : (i + 1) * Y2])
            p = H1 - 2 * h4 + 2 * i
            f1a[p] = f1a[p] + up
            f1a[p + 1] = f1a[p + 1] + up
        apply(1, f1a, g1, f1b, H1 - out0 - 2, H1 + B1 + out0 + 2)
        apply(1, f1b, g1, f1a, H1 - out0 - 1, H1 + B1 + out0 + 1)
        apply(1, f1a, g1, f1b, H1 - out0, H1 + B1 + out0)
        m = B1 + 2 * out0
        flat = dot(jnp.concatenate([f1b[H1 - out0 + i] for i in range(m)], axis=0), uz0)
        for i in range(m):
            up = dot(uy0, flat[i * Y1 : (i + 1) * Y1])
            p = HALO0 - 2 * out0 + 2 * i
            src[p] = src[p] + up
            src[p + 1] = src[p + 1] + up

    def at(h):
        return HALO0 - h, HALO0 + X + h

    def rest():
        each_b(far, hand_on, -1)
        each_b(far, lambda entry, dy: pass_b(entry, dy).wait_recv(), -1)
        low, high = HALO0, HALO0 + X
        apply(0, gk, gk, fb, low - 11, low - 2)
        apply(0, gk, gk, fb, high + 2, high + 11)
        apply(0, fb, gk, fa, low - 10, low - 1)
        apply(0, fb, gk, fa, high + 1, high + 10)

    apply(0, gk, gk, fb, *at(2))
    apply(0, fb, gk, fa, *at(1))
    coarse(0, fa, 5, rest)
    apply(0, fa, gk, fb, *at(9))
    apply(0, fb, gk, fa, *at(8))
    apply(0, fa, gk, fb, *at(7))
    apply(0, fb, gk, fa, *at(6))
    apply(0, fa, gk, fb, *at(5))
    apply(0, fb, gk, fa, *at(4))
    coarse(1, fa, 2, lambda: None)
    apply(0, fa, gk, fb, *at(3))
    apply(0, fb, gk, fa, *at(2))
    apply(0, fa, gk, fb, *at(1))

    acc = jnp.zeros((Y, Z), jnp.float32)
    r0, l0 = iotas((Y0, Z0))
    for i in range(X):
        p = HALO0 + i
        mid = fb[p]
        pot_ref[i] = own_lanes(own_rows(mid))
        j0 = 0.5 * own_lanes(own_rows(fb[p + 1] - fb[p - 1]))
        dy = jnp.where(r0 == Y0 - 1, 0.0, pltpu.roll(mid, Y0 - 1, 0)) - jnp.where(r0 == 0, 0.0, pltpu.roll(mid, 1, 0))
        dz = jnp.where(l0 == Z0 - 1, 0.0, pltpu.roll(mid, Z0 - 1, 1)) - jnp.where(l0 == 0, 0.0, pltpu.roll(mid, 1, 1))
        c0 = e_ref[0, i] - j0
        c1 = e_ref[1, i] - 0.5 * own_lanes(own_rows(dy))
        c2 = e_ref[2, i] - 0.5 * own_lanes(own_rows(dz))
        b0, b1, b2 = b_ref[0, i], b_ref[1, i], b_ref[2, i]
        m0 = v_ref[0, i] + section_weight * (c1 * b2 - c2 * b1)
        out_ref[0, i] = m0
        acc = acc + m0
        out_ref[1, i] = v_ref[1, i] + section_weight * (c2 * b0 - c0 * b2)
        out_ref[2, i] = v_ref[2, i] + section_weight * (c0 * b1 - c1 * b0)

    s1[...] = acc[:8] + acc[8:]
    pairs = [(dw, dt) for dw in range(CW) for dt in (0, 1)]

    def copy_p(k):
        dw, dt = pairs[k]
        return pltpu.make_async_remote_copy(
            s1, part1.at[k], sem_ps.at[k], sem_pr.at[k],
            device_id=(c, lax.rem(w + dw, CW), lax.rem(t + dt, 2)), device_id_type=MESH,
        )

    def copy_q(d):
        k = len(pairs) + d
        return pltpu.make_async_remote_copy(
            s2, part2.at[d], sem_ps.at[k], sem_pr.at[k],
            device_id=(lax.rem(c + d, CX), w, t), device_id_type=MESH,
        )

    for k in range(1, len(pairs)):
        copy_p(k).start()
    total = s1[...]
    for k in range(1, len(pairs)):
        copy_p(k).wait_recv()
        total = total + part1[k]
    s2[...] = total
    for d in range(1, CX):
        copy_q(d).start()
    for d in range(1, CX):
        copy_q(d).wait_recv()
        total = total + part2[d]
    bulk = jnp.sum(total) * (1.0 / float(nx0 * CW * Y * Z0))
    for i in range(X):
        out_ref[0, i] = out_ref[0, i] - bulk + cast_speed

    for k in range(4):
        pl.when(send_ok[k])(lambda k=k: copy_a(k).wait_send())
    copy_a(4).wait_send()
    each_b(steps, leave_b, 1)
    each_b(steps, lambda entry, dy: pass_b(entry, dy).wait_send(), -1)
    for n in range(CYCLES):
        each_c(n, lambda *a: copy_c(*a).wait_send(), 1, outward)
        each_c(n, lambda *a: pass_c(*a).wait_send(), -1, outward)
    for k in range(1, len(pairs)):
        copy_p(k).wait_send()
    for d in range(1, CX):
        copy_q(d).wait_send()


def solution(mesh):
    CX, CW = mesh.shape["cast"], mesh.shape["width"]

    def per_device(velocity, magnetic):
        _, X, Y, Z = velocity.shape
        two = CW == 2
        Y0 = 2 * Y if two else 3 * Y
        Y1 = Y if two else 5 * (Y // 2)
        Y2 = -(-(Y1 // 2) // 8) * 8
        Z0 = 2 * Z
        N0, N1, N2 = X + 2 * HALO0, (X // 2) * (2 * NEAR + 1), (X // 4) * (2 * NEAR + 1)
        nb, nc = 7 * (2 if two else 3), (2 * NEAR + 1) * (2 if two else 5)
        np_ = 2 * CW + CX
        f32 = jnp.float32
        V = pltpu.VMEM
        D = pltpu.SemaphoreType.DMA
        return pl.pallas_call(
            functools.partial(kernel, (CX, CW)),
            out_shape=(
                jax.ShapeDtypeStruct((3, X, Y, Z), f32),
                jax.ShapeDtypeStruct((X, Y, Z), f32),
            ),
            in_specs=[pl.BlockSpec(memory_space=V)] * 2,
            out_specs=(pl.BlockSpec(memory_space=V),) * 2,
            scratch_shapes=[
                V((3, X, Y, Z), f32), V((X, Y, Z), f32), V((Y, Z), f32), V((Y, Z), f32),
                V((2, X, Z), f32), V((2, X, Z), f32), V((X, Y, Z), f32),
                V((N0, Y0, Z0), f32), V((N0, Y0, Z0), f32), V((N0, Y0, Z0), f32),
                V((CYCLES, X // 2, Y // 2, Z), f32), V((CYCLES, N1, Y1, Z), f32),
                V((N1, Y1, Z), f32), V((N1, Y1, Z), f32), V((N1, Y1, Z), f32),
                V((N2, Y2, Z), f32), V((N2, Y2, Z), f32), V((N2, Y2, Z), f32),
                V((8, Z), f32), V((8, Z), f32), V((2 * CW, 8, Z), f32), V((CX, 8, Z), f32),
                D((5,)), D((5,)), D((2, nb)), D((2, nb)), D((CYCLES, 2, nc)), D((CYCLES, 2, nc)),
                D((np_,)), D((np_,)), D((1 + CYCLES,)),
            ],
            compiler_params=pltpu.CompilerParams(
                collective_id=0, has_side_effects=True, vmem_limit_bytes=40 * 1024 * 1024
            ),
        )(velocity, magnetic)

    placed = (P(None, "cast", "width", "thick"), P(None, "cast", "width", "thick"))
    return jax.shard_map(
        per_device,
        mesh=mesh,
        in_specs=placed,
        out_specs=(P(None, "cast", "width", "thick"), P("cast", "width", "thick")),
        check_vma=False,
    )
```

```python
import functools

import jax
import jax.numpy as jnp
from jax import lax
from jax.experimental import pallas as pl
from jax.experimental.pallas import tpu as pltpu
from jax.sharding import PartitionSpec as P

CYCLES = 2
weight = 0.8 / 6.0
keep = 0.2
section_weight = 0.5
cast_speed = 1.0
MESH = pl.DeviceIdType.MESH

HALO0 = 12
NEAR = 4


def pieces(a):
    high = a.astype(jnp.bfloat16)
    rest = a - high.astype(jnp.float32)
    mid = rest.astype(jnp.bfloat16)
    low = (rest - mid.astype(jnp.float32)).astype(jnp.bfloat16)
    return high, mid, low


def dot(a, b):
    if a.dtype == jnp.bfloat16:
        parts = [jnp.dot(a, q, preferred_element_type=jnp.float32) for q in pieces(b)]
    else:
        parts = [jnp.dot(q, b, preferred_element_type=jnp.float32) for q in pieces(a)]
    return parts[0] + (parts[1] + parts[2])


def iotas(shape):
    return lax.broadcasted_iota(jnp.int32, shape, 0), lax.broadcasted_iota(jnp.int32, shape, 1)


def pair_matrix(rows, cols, fine_axis, offset=0):
    i, j = iotas((rows, cols))
    if fine_axis == 0:
        hit = lax.shift_right_logical(i, 1) + offset == j
    else:
        hit = lax.shift_right_logical(j, 1) == i
    return jnp.where(hit, 1.0, 0.0).astype(jnp.bfloat16)


def kernel(
    counts, v_ref, b_ref, out_ref, pot_ref,
    e_ref, sblk, exl, exr, eys, eyn, ezp,
    gk, fa, fb, g1blk, g1w, f1a, f1b, r1, g2, f2a, f2b,
    s1, s2, part1, part2,
    sem_as, sem_ar, sem_bs, sem_br, sem_cs, sem_cr, sem_ps, sem_pr, sem_loc,
):
    CX, CW = counts
    X, Y, Z = sblk.shape
    Y0, Z0 = gk.shape[1], gk.shape[2]
    Y1, Y2 = g1w.shape[2], g2.shape[1]
    two = CW == 2
    c, w, t = lax.axis_index("cast"), lax.axis_index("width"), lax.axis_index("thick")
    nx0 = CX * X

    def has_x(d):
        return jnp.logical_and(c + d >= 0, c + d < CX)

    def has_w(d):
        return jnp.logical_and(w + d >= 0, w + d < CW)

    def dys(reach):
        return (0, 1) if two else tuple(range(-reach, reach + 1))

    def wid(dy):
        return lax.rem(w + dy, 2) if two else w + dy

    def when_x(dx, fn):
        if dx == 0:
            fn()
        else:
            pl.when(has_x(dx))(fn)

    def when_w(dy, fn):
        if dy == 0 or two:
            fn()
        else:
            pl.when(has_w(dy))(fn)

    for ref in (exl, exr, eyn):
        ref[...] = jnp.zeros_like(ref)

    def clear(ref, first, count, per):
        def body(i, carry):
            for j in range(per):
                ref[first + i * per + j] = jnp.zeros(ref.shape[1:], jnp.float32)
            return carry

        lax.fori_loop(0, count // per, body, 0)

    if not two:
        clear(gk, 0, gk.shape[0], 4)
        for n in range(CYCLES):
            clear(g1w.at[n], 0, g1w.shape[1], 4)

    barrier = pltpu.get_barrier_semaphore()
    need = jnp.int32(CX - 1)
    for d in range(1, CX):
        pl.semaphore_signal(barrier, 1, device_id=(lax.rem(c + d, CX), w, t), device_id_type=MESH)
    all_w = (0, 1) if two else tuple(range(-(CW - 1), CW))
    far = NEAR
    for dx in range(-far, far + 1):
        for dy in all_w:
            for dt in (0, 1):
                if dy == 0 and dt == 0:
                    continue
                near = dt == 0 and (two or abs(dy) <= 2)
                if not (near or dx == 0):
                    continue
                ok = jnp.bool_(True)
                if dx:
                    ok = jnp.logical_and(ok, has_x(dx))
                if dy and not two:
                    ok = jnp.logical_and(ok, has_w(dy))

                def greet(dx=dx, dy=dy, dt=dt):
                    pl.semaphore_signal(
                        barrier, 1, device_id=(c + dx, wid(dy), lax.rem(t + dt, 2)), device_id_type=MESH
                    )

                if dx == 0 and (dy == 0 or two):
                    greet()
                    need = need + 1
                else:
                    pl.when(ok)(greet)
                    need = need + jnp.where(ok, 1, 0).astype(jnp.int32)

    if two:
        @pl.when(jnp.logical_not(has_x(-2)))
        def _():
            clear(gk, 0, 4, 4)

        @pl.when(jnp.logical_not(has_x(-1)))
        def _():
            clear(gk, 4, 8, 4)

        @pl.when(jnp.logical_not(has_x(1)))
        def _():
            clear(gk, 20, 8, 4)

        @pl.when(jnp.logical_not(has_x(2)))
        def _():
            clear(gk, 28, 4, 4)

        for n in range(CYCLES):
            for dx in range(-NEAR, NEAR + 1):
                if dx:
                    @pl.when(jnp.logical_not(has_x(dx)))
                    def _(n=n, dx=dx):
                        clear(g1w.at[n], 4 * (NEAR + dx), 4, 4)

    for i in range(X):
        v0, v1, v2 = v_ref[0, i], v_ref[1, i], v_ref[2, i]
        b0, b1, b2 = b_ref[0, i], b_ref[1, i], b_ref[2, i]
        e_ref[0, i] = v1 * b2 - v2 * b1
        ey = v2 * b0 - v0 * b2
        e_ref[1, i] = ey
        eys[0, i : i + 1, :] = ey[0:1, :]
        eys[1, i : i + 1, :] = ey[Y - 1 : Y, :]
        e_ref[2, i] = v0 * b1 - v1 * b0

    pl.semaphore_wait(barrier, need)

    def copy_a(k):
        if k == 0:
            args = (e_ref.at[0, X - 1], exl, (c + 1, w, t))
        elif k == 1:
            args = (e_ref.at[0, 0], exr, (c - 1, w, t))
        elif k == 2:
            args = (eys.at[1], eyn.at[0], (c, w + 1, t))
        elif k == 3:
            args = (eys.at[0], eyn.at[1], (c, w - 1, t))
        else:
            args = (e_ref.at[2], ezp, (c, w, 1 - t))
        return pltpu.make_async_remote_copy(
            args[0], args[1], sem_as.at[k], sem_ar.at[k], device_id=args[2], device_id_type=MESH
        )

    send_ok = (has_x(1), has_x(-1), has_w(1), has_w(-1))
    recv_ok = (has_x(-1), has_x(1), has_w(-1), has_w(1))
    for k in range(4):
        pl.when(send_ok[k])(lambda k=k: copy_a(k).start())
    copy_a(4).start()
    for k in range(4):
        pl.when(recv_ok[k])(lambda k=k: copy_a(k).wait_recv())
    copy_a(4).wait_recv()

    row, lane = iotas((Y, Z))
    for i in range(X):
        ex0 = e_ref[0, i - 1] if i else exl[...]
        ex1 = e_ref[0, i + 1] if i < X - 1 else exr[...]
        ey, ez, pz = e_ref[1, i], e_ref[2, i], ezp[i]
        ey1 = jnp.where(row == Y - 1, eyn[1, i : i + 1, :], pltpu.roll(ey, Y - 1, 0))
        ey0 = jnp.where(row == 0, eyn[0, i : i + 1, :], pltpu.roll(ey, 1, 0))
        edge1 = jnp.where(t == 0, pltpu.roll(pz, Z - 1, 1), 0.0)
        edge0 = jnp.where(t == 0, 0.0, pltpu.roll(pz, 1, 1))
        ez1 = jnp.where(lane == Z - 1, edge1, pltpu.roll(ez, Z - 1, 1))
        ez0 = jnp.where(lane == 0, edge0, pltpu.roll(ez, 1, 1))
        sblk[i] = (-0.5 * weight) * ((ex1 - ex0) + (ey1 - ey0) + (ez1 - ez0))

    def rows_b(dy):
        return pl.ds(pl.multiple_of(w * Y, Y), Y) if two else pl.ds((1 - dy) * Y, Y)

    my_lanes = pl.ds(pl.multiple_of(t * Z, Z), Z)
    ydys = dys(1)
    other = (c, w, 1 - t)
    mid = [(0, 0, X, HALO0)]
    near = mid + [(1, X - 4, 4, HALO0 - 4), (-1, 0, 4, HALO0 + X)]
    far = [
        (1, 0, 4, HALO0 - 8), (-1, X - 4, 4, HALO0 + X + 4),
        (2, X - 4, 4, HALO0 - 12), (-2, 0, 4, HALO0 + X + 8),
    ]
    steps = near + far

    def slot_b(entry, dy):
        return steps.index(entry) * len(ydys) + ydys.index(dy)

    def rows_in(dy, size, reach):
        return pl.ds(pl.multiple_of(wid(dy) * size, size), size) if two else pl.ds((reach - dy) * size, size)

    def copy_b(entry, dy):
        dx, first, count, land = entry
        k = slot_b(entry, dy)
        return pltpu.make_async_remote_copy(
            sblk.at[pl.ds(first, count)],
            gk.at[pl.ds(land, count), rows_b(dy), my_lanes],
            sem_bs.at[0, k], sem_br.at[0, k],
            device_id=(c + dx, wid(dy), t), device_id_type=MESH,
        )

    def pass_b(entry, dy):
        _, _, count, land = entry
        k = slot_b(entry, dy)
        place = gk.at[pl.ds(land, count), rows_in(dy, Y, 1), my_lanes]
        src = sblk if entry[0] == 0 and dy == 0 else place
        return pltpu.make_async_remote_copy(
            src, place, sem_bs.at[1, k], sem_br.at[1, k], device_id=other, device_id_type=MESH
        )

    def each_b(entries, fn, sign):
        for entry in entries:
            def run(entry=entry):
                for dy in ydys:
                    when_w(sign * dy, lambda dy=dy: fn(entry, dy))

            when_x(sign * entry[0], run)

    def is_own(entry, dy):
        return entry[0] == 0 and dy == 0

    def start_b(entry, dy):
        if not is_own(entry, dy):
            copy_b(entry, dy).start()

    def hand_on(entry, dy):
        if not is_own(entry, dy):
            copy_b(entry, dy).wait_recv()
            pass_b(entry, dy).start()

    def leave_b(entry, dy):
        if not is_own(entry, dy):
            copy_b(entry, dy).wait_send()

    each_b(steps, start_b, 1)
    pass_b(mid[0], 0).start()
    own = pltpu.make_async_copy(
        sblk, gk.at[pl.ds(HALO0, X), pl.ds(pl.multiple_of(w * Y, Y), Y) if two else pl.ds(Y, Y), my_lanes],
        sem_loc.at[0],
    )
    own.start()
    own.wait()
    each_b(near, hand_on, -1)
    each_b(near, lambda entry, dy: pass_b(entry, dy).wait_recv(), -1)

    def neighbours(v):
        ny, nz = v.shape
        r, l = iotas(v.shape)
        total = jnp.where(r == 0, 0.0, pltpu.roll(v, 1, 0)) + jnp.where(r == ny - 1, 0.0, pltpu.roll(v, ny - 1, 0))
        total = total + jnp.where(l == 0, 0.0, pltpu.roll(v, 1, 1))
        return total + jnp.where(l == nz - 1, 0.0, pltpu.roll(v, nz - 1, 1))

    def factor(plane, first, count, shape, lev):
        g = first + plane
        k = jnp.where(jnp.logical_and(g >= 0, g < count), weight, 0.0).astype(jnp.float32)
        if not two:
            base = (w * Y - Y, w * (Y // 2) - Y, w * (Y // 4) - Y // 2)[lev]
            size = (CW * Y, CW * (Y // 2), CW * (Y // 4))[lev]
            r, _ = iotas(shape)
            k = jnp.where(jnp.logical_and(r + base >= 0, r + base < size), k, 0.0)
        if lev == 2:
            _, l = iotas(shape)
            k = jnp.where(l < Z0 // 4, k, 0.0)
        return k

    def apply(lev, src, g, dst, lo, hi, residual=False, last=None):
        first = (c * X - HALO0, c * (X // 2) - NEAR * (X // 2), c * (X // 4) - NEAR * (X // 4))[lev]
        count = nx0 >> lev
        n = hi - lo
        step = max(d for d in range(1, 14 if lev == 0 else 18) if n % d == 0)

        def body(i, carry):
            p = lo + i * step
            v = [src[p - 1 + j] for j in range(step + 2)]
            for j in range(step):
                mid = v[j + 1]
                nb = v[j] + v[j + 2] + neighbours(mid)
                k = factor(p + j, first, count, mid.shape, lev)
                if residual:
                    dst[p + j] = g[p + j] + k * nb - 0.8 * mid
                else:
                    dst[p + j] = keep * mid + k * nb + g[p + j]
            return carry

        lax.fori_loop(0, n // step, body, 0)

    def own_rows(v):
        return jnp.where(w == 0, v[:Y], v[Y:]) if two else v[Y : 2 * Y]

    def own_lanes(v):
        return jnp.where(t == 0, v[:, :Z], v[:, Z:])

    H1 = NEAR * (X // 2)
    H2 = NEAR * (X // 4)
    pz0 = pair_matrix(Z0, Z0 // 2, 0)
    pz1 = pair_matrix(Z0 // 2, Z0 // 2, 0)
    uz0 = pair_matrix(Z0 // 2, Z0, 1)
    uz1 = pair_matrix(Z0 // 2, Z0 // 2, 1)
    py0 = pair_matrix(Y // 2, Y, 1)
    py1 = pair_matrix(Y2, Y1, 1)
    uy1 = pair_matrix(Y1, Y2, 0)
    uy0 = pair_matrix(Y0, Y1, 0, 0 if two else Y // 2)

    cdys = dys(2)

    def rows_c(dy):
        half = Y // 2
        return pl.ds(pl.multiple_of(w * half, half), half) if two else pl.ds((2 - dy) * half, half)

    part = X // 4

    def copy_c(n, dx, dy):
        k = (dx + NEAR) * len(cdys) + cdys.index(dy)
        return pltpu.make_async_remote_copy(
            g1blk.at[n, pl.ds(t * part, part)],
            g1w.at[n, pl.ds((NEAR - dx) * (X // 2) + t * part, part), rows_c(dy)],
            sem_cs.at[n, 0, k], sem_cr.at[n, 0, k],
            device_id=(c + dx, wid(dy), t), device_id_type=MESH,
        )

    def pass_c(n, dx, dy):
        k = (dx + NEAR) * len(cdys) + cdys.index(dy)
        place = g1w.at[n, pl.ds((NEAR - dx) * (X // 2) + t * part, part), rows_in(dy, Y // 2, 2)]
        return pltpu.make_async_remote_copy(
            place, place, sem_cs.at[n, 1, k], sem_cr.at[n, 1, k], device_id=other, device_id_type=MESH
        )

    def each_c(n, fn, sign, order):
        for dx in order:
            def run(dx=dx):
                for dy in cdys:
                    if dx or dy:
                        when_w(sign * dy, lambda dy=dy: fn(n, dx, dy))

            when_x(sign * dx, run)

    outward = (0, 1, -1, 2, -2, 3, -3, 4, -4)

    def hand_on_c(n, dx, dy):
        copy_c(n, dx, dy).wait_recv()
        pass_c(n, dx, dy).start()

    def coarse(n, src, out0, between):
        apply(0, src, gk, fb, HALO0, HALO0 + X, residual=True)
        sums = [own_rows(fb[HALO0 + 2 * i] + fb[HALO0 + 2 * i + 1]) for i in range(X // 2)]
        flat = 0.5 * dot(jnp.concatenate(sums, axis=0), pz0)
        for i in range(X // 2):
            g1blk[n, i] = dot(py0, flat[i * Y : (i + 1) * Y])
        each_c(n, lambda *a: copy_c(*a).start(), 1, outward[::-1])
        mine = pltpu.make_async_copy(
            g1blk.at[n], g1w.at[n, pl.ds(H1, X // 2), rows_c(0)], sem_loc.at[1 + n]
        )
        mine.start()
        mine.wait()
        between()
        each_c(n, hand_on_c, -1, outward)
        each_c(n, lambda *a: pass_c(*a).wait_recv(), -1, outward)

        g1 = g1w.at[n]
        B1, B2 = X // 2, X // 4
        h8 = out0 + 3
        h4 = (h8 + 1) // 2
        h6 = h4 + 2
        h12 = 2 * h6
        apply(1, g1, g1, f1b, H1 - h12 - 2, H1 + B1 + h12 + 2)
        apply(1, f1b, g1, f1a, H1 - h12 - 1, H1 + B1 + h12 + 1)
        apply(1, f1a, g1, r1, H1 - h12, H1 + B1 + h12, residual=True)
        m = B2 + 2 * h6
        lo = H1 - h12
        half = [r1[lo + 2 * i] + r1[lo + 2 * i + 1] for i in range(m)]
        flat = 0.5 * dot(jnp.concatenate(half, axis=0), pz1)
        for i in range(m):
            g2[H2 - h6 + i] = dot(py1, flat[i * Y1 : (i + 1) * Y1])
        apply(2, g2, g2, f2b, H2 - h6 + 1, H2 + B2 + h6 - 1)
        apply(2, f2b, g2, f2a, H2 - h4, H2 + B2 + h4)
        m = B2 + 2 * h4
        flat = dot(jnp.concatenate([f2a[H2 - h4 + i] for i in range(m)], axis=0), uz1)
        for i in range(m):
            up = dot(uy1, flat[i * Y2 : (i + 1) * Y2])
            p = H1 - 2 * h4 + 2 * i
            f1a[p] = f1a[p] + up
            f1a[p + 1] = f1a[p + 1] + up
        apply(1, f1a, g1, f1b, H1 - out0 - 2, H1 + B1 + out0 + 2)
        apply(1, f1b, g1, f1a, H1 - out0 - 1, H1 + B1 + out0 + 1)
        apply(1, f1a, g1, f1b, H1 - out0, H1 + B1 + out0)
        m = B1 + 2 * out0
        flat = dot(jnp.concatenate([f1b[H1 - out0 + i] for i in range(m)], axis=0), uz0)
        for i in range(m):
            up = dot(uy0, flat[i * Y1 : (i + 1) * Y1])
            p = HALO0 - 2 * out0 + 2 * i
            src[p] = src[p] + up
            src[p + 1] = src[p + 1] + up

    def at(h):
        return HALO0 - h, HALO0 + X + h

    def rest():
        each_b(far, hand_on, -1)
        each_b(far, lambda entry, dy: pass_b(entry, dy).wait_recv(), -1)
        low, high = HALO0, HALO0 + X
        apply(0, gk, gk, fb, low - 11, low - 2)
        apply(0, gk, gk, fb, high + 2, high + 11)
        apply(0, fb, gk, fa, low - 10, low - 1)
        apply(0, fb, gk, fa, high + 1, high + 10)

    apply(0, gk, gk, fb, *at(2))
    apply(0, fb, gk, fa, *at(1))
    coarse(0, fa, 5, rest)
    apply(0, fa, gk, fb, *at(9))
    apply(0, fb, gk, fa, *at(8))
    apply(0, fa, gk, fb, *at(7))
    def outer():
        low, high = HALO0, HALO0 + X
        for src, dst, h in ((fb, fa, 6), (fa, fb, 5), (fb, fa, 4)):
            apply(0, src, gk, dst, low - h, low - h + 3)
            apply(0, src, gk, dst, high + h - 3, high + h)

    apply(0, fb, gk, fa, *at(3))
    apply(0, fa, gk, fb, *at(2))
    apply(0, fb, gk, fa, *at(1))
    coarse(1, fa, 2, outer)
    apply(0, fa, gk, fb, *at(3))
    apply(0, fb, gk, fa, *at(2))
    apply(0, fa, gk, fb, *at(1))

    acc = jnp.zeros((Y, Z), jnp.float32)
    r0, l0 = iotas((Y0, Z0))
    for i in range(X):
        p = HALO0 + i
        mid = fb[p]
        pot_ref[i] = own_lanes(own_rows(mid))
        j0 = 0.5 * own_lanes(own_rows(fb[p + 1] - fb[p - 1]))
        dy = jnp.where(r0 == Y0 - 1, 0.0, pltpu.roll(mid, Y0 - 1, 0)) - jnp.where(r0 == 0, 0.0, pltpu.roll(mid, 1, 0))
        dz = jnp.where(l0 == Z0 - 1, 0.0, pltpu.roll(mid, Z0 - 1, 1)) - jnp.where(l0 == 0, 0.0, pltpu.roll(mid, 1, 1))
        c0 = e_ref[0, i] - j0
        c1 = e_ref[1, i] - 0.5 * own_lanes(own_rows(dy))
        c2 = e_ref[2, i] - 0.5 * own_lanes(own_rows(dz))
        b0, b1, b2 = b_ref[0, i], b_ref[1, i], b_ref[2, i]
        m0 = v_ref[0, i] + section_weight * (c1 * b2 - c2 * b1)
        out_ref[0, i] = m0
        acc = acc + m0
        out_ref[1, i] = v_ref[1, i] + section_weight * (c2 * b0 - c0 * b2)
        out_ref[2, i] = v_ref[2, i] + section_weight * (c0 * b1 - c1 * b0)

    s1[...] = acc[:8] + acc[8:]
    pairs = [(dw, dt) for dw in range(CW) for dt in (0, 1)]

    def copy_p(k):
        dw, dt = pairs[k]
        return pltpu.make_async_remote_copy(
            s1, part1.at[k], sem_ps.at[k], sem_pr.at[k],
            device_id=(c, lax.rem(w + dw, CW), lax.rem(t + dt, 2)), device_id_type=MESH,
        )

    def copy_q(d):
        k = len(pairs) + d
        return pltpu.make_async_remote_copy(
            s2, part2.at[d], sem_ps.at[k], sem_pr.at[k],
            device_id=(lax.rem(c + d, CX), w, t), device_id_type=MESH,
        )

    for k in range(1, len(pairs)):
        copy_p(k).start()
    total = s1[...]
    for k in range(1, len(pairs)):
        copy_p(k).wait_recv()
        total = total + part1[k]
    s2[...] = total
    for d in range(1, CX):
        copy_q(d).start()
    for d in range(1, CX):
        copy_q(d).wait_recv()
        total = total + part2[d]
    bulk = jnp.sum(total) * (1.0 / float(nx0 * CW * Y * Z0))
    for i in range(X):
        out_ref[0, i] = out_ref[0, i] - bulk + cast_speed

    for k in range(4):
        pl.when(send_ok[k])(lambda k=k: copy_a(k).wait_send())
    copy_a(4).wait_send()
    each_b(steps, leave_b, 1)
    each_b(steps, lambda entry, dy: pass_b(entry, dy).wait_send(), -1)
    for n in range(CYCLES):
        each_c(n, lambda *a: copy_c(*a).wait_send(), 1, outward)
        each_c(n, lambda *a: pass_c(*a).wait_send(), -1, outward)
    for k in range(1, len(pairs)):
        copy_p(k).wait_send()
    for d in range(1, CX):
        copy_q(d).wait_send()


def solution(mesh):
    CX, CW = mesh.shape["cast"], mesh.shape["width"]

    def per_device(velocity, magnetic):
        _, X, Y, Z = velocity.shape
        two = CW == 2
        Y0 = 2 * Y if two else 3 * Y
        Y1 = Y if two else 5 * (Y // 2)
        Y2 = -(-(Y1 // 2) // 8) * 8
        Z0 = 2 * Z
        N0, N1, N2 = X + 2 * HALO0, (X // 2) * (2 * NEAR + 1), (X // 4) * (2 * NEAR + 1)
        nb, nc = 7 * (2 if two else 3), (2 * NEAR + 1) * (2 if two else 5)
        np_ = 2 * CW + CX
        f32 = jnp.float32
        V = pltpu.VMEM
        D = pltpu.SemaphoreType.DMA
        return pl.pallas_call(
            functools.partial(kernel, (CX, CW)),
            out_shape=(
                jax.ShapeDtypeStruct((3, X, Y, Z), f32),
                jax.ShapeDtypeStruct((X, Y, Z), f32),
            ),
            in_specs=[pl.BlockSpec(memory_space=V)] * 2,
            out_specs=(pl.BlockSpec(memory_space=V),) * 2,
            scratch_shapes=[
                V((3, X, Y, Z), f32), V((X, Y, Z), f32), V((Y, Z), f32), V((Y, Z), f32),
                V((2, X, Z), f32), V((2, X, Z), f32), V((X, Y, Z), f32),
                V((N0, Y0, Z0), f32), V((N0, Y0, Z0), f32), V((N0, Y0, Z0), f32),
                V((CYCLES, X // 2, Y // 2, Z), f32), V((CYCLES, N1, Y1, Z), f32),
                V((N1, Y1, Z), f32), V((N1, Y1, Z), f32), V((N1, Y1, Z), f32),
                V((N2, Y2, Z), f32), V((N2, Y2, Z), f32), V((N2, Y2, Z), f32),
                V((8, Z), f32), V((8, Z), f32), V((2 * CW, 8, Z), f32), V((CX, 8, Z), f32),
                D((5,)), D((5,)), D((2, nb)), D((2, nb)), D((CYCLES, 2, nc)), D((CYCLES, 2, nc)),
                D((np_,)), D((np_,)), D((1 + CYCLES,)),
            ],
            compiler_params=pltpu.CompilerParams(
                collective_id=0, has_side_effects=True, vmem_limit_bytes=40 * 1024 * 1024
            ),
        )(velocity, magnetic)

    placed = (P(None, "cast", "width", "thick"), P(None, "cast", "width", "thick"))
    return jax.shard_map(
        per_device,
        mesh=mesh,
        in_specs=placed,
        out_specs=(P(None, "cast", "width", "thick"), P("cast", "width", "thick")),
        check_vma=False,
    )
```
